32 devices in a mesh: grp: 2 (over x), rad: 8 (over z, y), chan: 2 (over core).
Axes of the slice: x: 2, y: 2, z: 4, core: 2. Of those that a mesh axis runs over, the one named last changes fastest.
Arguments:
- wave: bfloat16 [64, 2, 240, 1024], P('chan', None, 'rad', 'grp'), parts along dimension 3, may hold values from -6 to 6
- tile_elems: int32 [16], P(('grp', 'rad')), parts along dimension 0, may hold values from 1 to 2, 12 in all
- element_width: float32 [24], P('grp'), parts along dimension 0, may hold values from 0.7 to 1.4
- element_kinetic: float32 [16, 16], replicated, may hold values from -0.2 to 2, as said below
- radial_two: float32 [512, 512], replicated, may hold values from -1 to 4, as said below
- angular: float32 [2, 64, 64], replicated, may hold values from -24 to 24
- channel_table: int32 [64, 2], replicated, may hold values from 0 to 11, as said below
Outputs:
- evolved: float32 [64, 2, 240, 1024], P('chan', None, 'rad', 'grp'), parts along dimension 3
The draws below stay inside these ranges and needn't reach their ends.
There are 2 independent parts, one for each index of `grp`. The reference program is written for one: setup_inputs(seed, part) draws one part's arguments, and reference() takes and returns one part's arrays. A program takes and returns all parts, laid end to end along the dimension named above; an argument that names none is the same for every part. Nothing has to cross between parts.
Inputs may be any that keep to these rules, and one draw needn't show every extreme that they name: `tile_elems`: the counts of one part sum to 12; some tile holds exactly 2 elements. `channel_table`: each row is a pair (l1, l2) of angular momenta; no two rows are equal; the pair (11, 11) is present. `element_kinetic`: A symmetric matrix. `radial_two`: A symmetric matrix.
All inputs are finite; a program needn't handle non-finite values. No bound on the sum of `tile_elems` on one device may be relied on, other than what follows from the above.
Results may differ from the reference program's by a relative error of at most 0.0003.
Values may be sent and summed in bfloat16 or wider, within the bound.
A program may use at most 64 MiB of HBM per device.

```python
import math
import jax
import jax.numpy as jnp
import numpy as np
from jax import lax

NCH = 64
LMAX = 12
LAM = 2
PTS = 15
SLOTS = 2
R2 = 512
STEPS = 1
ORDER = 1
N1 = 240
TOTAL_ELEMS = 12
N_RAD = 8


def draw_element_kinetic(key, part):
    first_key, second_key = jax.random.split(jax.random.fold_in(key, 5))
    raw_values = jax.random.uniform(first_key, (PTS + 1, PTS + 1), jnp.float32, -0.1, 0.1)
    diagonal_part = jax.random.uniform(second_key, (PTS + 1,), jnp.float32, 1.5, 2.0)
    identity = jnp.eye(PTS + 1, dtype=jnp.float32)
    return (raw_values + raw_values.T) * (1.0 - identity) + identity * diagonal_part[None, :]


def draw_radial_two(key, part):
    first_key, second_key = jax.random.split(jax.random.fold_in(key, 11))
    edge_bound = 1.22 / math.sqrt(R2)
    raw_values = jax.random.uniform(first_key, (R2, R2), jnp.float32, -edge_bound, edge_bound)
    diagonal_part = jax.random.uniform(second_key, (R2,), jnp.float32, 3.0, 4.0)
    identity = jnp.eye(R2, dtype=jnp.float32)
    return (raw_values + raw_values.T) * (1.0 - identity) + identity * diagonal_part[None, :]


def draw_channel_table(key, part):
    first_key, second_key = jax.random.split(jax.random.fold_in(key, 7))
    chosen = jax.random.permutation(first_key, LMAX * LMAX - 1)[:NCH - 1]
    values = jnp.concatenate([chosen, jnp.full((1,), LMAX * LMAX - 1, dtype=chosen.dtype)]).astype(jnp.int32)
    values = jax.random.permutation(second_key, values)
    return jnp.stack([values // LMAX, values % LMAX], axis=1).astype(jnp.int32)


def block_scale(stream_key, dims, pieces, low, top_value):
    def one(dim, blocks):
        steps = jax.random.uniform(jax.random.fold_in(jax.random.fold_in(stream_key, 6), dim), (blocks,), jnp.float32, low / len(pieces), top_value / len(pieces))
        return jnp.repeat(jnp.exp(steps), dims[dim] // blocks).reshape((-1,) + (1,) * (len(dims) - dim - 1))

    factor_of = one(*pieces[0])
    for cut in pieces[1:]:
        factor_of = factor_of * one(*cut)
    return factor_of


def length_profile(count, total, reach, slope):
    loads = [(1 << 20) // math.isqrt(rank ** slope) + 1 for rank in range(2, count + 1)]
    rest, holding = total - reach - (count - 1), [1] * (count - 1)
    while rest > 0:
        candidates = [i for i in range(count - 1) if holding[i] < reach]
        whole, remaining = sum([loads[i] for i in candidates]), rest
        for i in candidates:
            addition = min(reach - holding[i], max(1, remaining * loads[i] // whole), rest)
            holding[i] = holding[i] + addition
            rest = rest - addition
    return np.array([reach] + holding)


def ragged(rng, count, total, limit, skew):
    if count == 2:
        one = jax.random.randint(rng, (), max(1, total - limit), min(limit, total - 1) + 1)
        return jnp.stack([one, total - one])
    sizes = jnp.asarray(length_profile(count, total, limit, skew), jnp.int32)
    twos = (count - 1) // 2
    giver, sink = sizes[1:1 + 2 * twos:2], sizes[2:2 + 2 * twos:2]
    slack = jnp.minimum(giver - 1, limit - sink)
    moved = jax.random.randint(jax.random.fold_in(rng, 1), (twos,), 0, 1 << 20) % (slack + 1)
    sizes = sizes.at[1:1 + 2 * twos:2].set(giver - moved).at[2:2 + 2 * twos:2].set(sink + moved)
    return sizes[jax.random.permutation(jax.random.fold_in(rng, 2), count)]


def scatter_about(rng, shape, deviation, bound, pieces=(), held_as=jnp.bfloat16):
    values = deviation * jax.random.normal(rng, shape, jnp.float32)
    if pieces:
        values = values * block_scale(rng, shape, pieces, -0.22, 0.18)
    return jnp.clip(values, -bound, bound).astype(held_as)


def setup_inputs(seed: int = 0, part: int = 0) -> dict:
    keys = jax.random.split(jax.random.key(seed), 8)
    part_splits = jax.random.split(jax.random.fold_in(keys[7], part), 8)
    wave = scatter_about(part_splits[0], (NCH, 2, N1, R2), 1.0, 6.0, ((0, 2), (2, 8)))
    tile_elems = ragged(part_splits[1], N_RAD, TOTAL_ELEMS, SLOTS, 2).astype(jnp.int32)
    element_width = jnp.clip(jnp.exp(jax.random.uniform(part_splits[2], (TOTAL_ELEMS,), jnp.float32, math.log(0.7), math.log(1.4))), 0.7, 1.4)
    element_kinetic = draw_element_kinetic(jax.random.fold_in(keys[7], 71), part)
    radial_two = draw_radial_two(jax.random.fold_in(keys[7], 71), part)
    angular = scatter_about(keys[5], (LAM, NCH, NCH), 6.0, 24.0, (), jnp.float32)
    channel_table = draw_channel_table(jax.random.fold_in(keys[7], 71), part)
    return dict(wave=wave, tile_elems=tile_elems, element_width=element_width, element_kinetic=element_kinetic, radial_two=radial_two, angular=angular, channel_table=channel_table)


highest = lax.Precision.HIGHEST
charge = 2.0
inner_radius = 4.0
radial_step = 0.1
time_step = 0.1


def node_fractions():
    points = jnp.arange(PTS, dtype=jnp.float32)
    return 0.5 * (1.0 - jnp.cos(jnp.pi * points / PTS))


def allowed_pairs(orbital_a, orbital_b, multipole):
    lower_bound = jnp.abs(orbital_a[:, None] - orbital_b[None, :])
    upper_bound = orbital_a[:, None] + orbital_b[None, :]
    return (lower_bound <= multipole) & (multipole <= upper_bound) & ((upper_bound + multipole) % 2 == 0)


def couplings(angular, channel_table):
    orbital_first = channel_table[:, 0]
    orbital_second = channel_table[:, 1]
    matrices = []
    for multipole in range(LAM):
        selected = allowed_pairs(orbital_first, orbital_first, multipole) & allowed_pairs(orbital_second, orbital_second, multipole)
        symmetric = 0.5 * (angular[multipole] + angular[multipole].T)
        matrices.append(jnp.where(selected, symmetric, 0.0))
    return jnp.stack(matrices)


def radial_weights(r_one, r_two):
    nearer = jnp.minimum(r_one[..., None], r_two)
    farther = jnp.maximum(r_one[..., None], r_two)
    return jnp.stack([nearer ** multipole / farther ** (multipole + 1) for multipole in range(LAM)])


def diagonal_terms(table_rows, r_one, r_two):
    orbital_first = table_rows[:, 0].astype(jnp.float32)
    orbital_second = table_rows[:, 1].astype(jnp.float32)
    centri_first = 0.5 * orbital_first * (orbital_first + 1.0)
    centri_second = 0.5 * orbital_second * (orbital_second + 1.0)
    inv_one = 1.0 / r_one
    inv_two = 1.0 / r_two
    angular_part = centri_first[:, None, None, None] * (inv_one * inv_one)[None, :, :, None] + centri_second[:, None, None, None] * (inv_two * inv_two)
    return angular_part - charge * (inv_one[None, :, :, None] + inv_two)


def propagate(field, apply_ham):
    for step_index in range(STEPS):
        taylor_term = field
        running = field
        for term_order in range(1, ORDER + 1):
            applied = apply_ham(taylor_term)
            taylor_term = (time_step / term_order) * jnp.stack([applied[:, 1], -applied[:, 0]], axis=1)
            running = running + taylor_term
        field = running
    return field


def reference(wave, tile_elems, element_width, element_kinetic, radial_two, angular, channel_table):
    offsets = jnp.cumsum(tile_elems) - tile_elems
    elements = jnp.arange(TOTAL_ELEMS, dtype=jnp.int32)
    owner_tile = jnp.sum((offsets[None, :] <= elements[:, None]).astype(jnp.int32), axis=1) - 1
    slot_index = elements - offsets[owner_tile]
    padded = (owner_tile * SLOTS + slot_index).astype(jnp.int32)
    padded_grid = wave.astype(jnp.float32).reshape(NCH, 2, N_RAD * SLOTS, PTS, R2)
    field = padded_grid[:, :, padded]
    starts_all = jnp.concatenate([jnp.zeros((1,), jnp.float32), jnp.cumsum(element_width)])[:TOTAL_ELEMS]
    r_one = inner_radius + starts_all[:, None] + element_width[:, None] * node_fractions()[None, :]
    r_two = inner_radius + radial_step * jnp.arange(R2, dtype=jnp.float32)
    kinetic = element_kinetic[None] / (element_width * element_width)[:, None, None]
    coupling_mats = couplings(angular, channel_table)
    weights = radial_weights(r_one, r_two)
    potential = diagonal_terms(channel_table, r_one, r_two)

    def apply_ham(values):
        zero_row = jnp.zeros_like(values[:, :, :1, :1, :])
        next_rows = jnp.concatenate([values[:, :, 1:, :1, :], zero_row], axis=2)
        block = jnp.concatenate([values, next_rows], axis=3)
        element_out = jnp.einsum('gqp,cxgpr->cxgqr', kinetic, block, precision=highest)
        result = element_out[:, :, :, :PTS, :]
        result = result.at[:, :, 1:, 0, :].add(element_out[:, :, :-1, PTS, :])
        result = result + jnp.einsum('cxgpr,rs->cxgps', values, radial_two, precision=highest)
        result = result + potential[:, None] * values
        for multipole in range(LAM):
            result = result + jnp.einsum('cd,dxgpr->cxgpr', coupling_mats[multipole], weights[multipole] * values, precision=highest)
        return result

    evolved = propagate(field, apply_ham)
    output = jnp.zeros_like(padded_grid).at[:, :, padded].set(evolved)
    return output.reshape(wave.shape)
```

```python
import functools

import jax
import jax.numpy as jnp
from jax import lax
from jax.experimental import pallas as pl
from jax.experimental.pallas import tpu as pltpu
from jax.sharding import PartitionSpec as P

PTS = 15
SLOTS = 2
MESH = pl.DeviceIdType.MESH
highest = lax.Precision.HIGHEST
charge = 2.0
inner_radius = 4.0
radial_step = 0.1
time_step = 0.1


def mm(a, b):
    return jnp.dot(a, b, preferred_element_type=jnp.float32)


def two_parts(a):
    high = a.astype(jnp.bfloat16)
    return high, (a - high.astype(jnp.float32)).astype(jnp.bfloat16)


def kron_parts(small, outer, inner, small_outer):
    size = outer * inner
    width = small.shape[0]
    row = lax.broadcasted_iota(jnp.int32, (size, width), 0)
    col = lax.broadcasted_iota(jnp.int32, (size, width), 1)
    pick_r = ((row // inner if small_outer else row % inner) == col).astype(jnp.float32)
    row = lax.broadcasted_iota(jnp.int32, (width, size), 0)
    col = lax.broadcasted_iota(jnp.int32, (width, size), 1)
    pick_c = ((col // inner if small_outer else col % inner) == row).astype(jnp.float32)
    spread = jnp.dot(pick_r, small, precision=highest, preferred_element_type=jnp.float32)
    spread = jnp.dot(spread, pick_c, precision=highest, preferred_element_type=jnp.float32)
    row = lax.broadcasted_iota(jnp.int32, (size, size), 0)
    col = lax.broadcasted_iota(jnp.int32, (size, size), 1)
    keep = (row % inner == col % inner) if small_outer else (row // inner == col // inner)
    return two_parts(jnp.where(keep, spread, 0.0))


def kernel(
    n_rad, v, count, widths, fractions, kin_s, kin_v, rtwo, m_own, m_oth, coef, out,
    other, next_in, below, spill, counts, kin, acc,
    c_send, c_recv, k_send, k_recv, e_send, e_recv,
):
    channels, width_two = v.shape[2], v.shape[3]
    me_rad = lax.axis_index("rad")
    me_chan = lax.axis_index("chan")
    partner = 1 - me_chan
    rad_of = [lax.rem(me_rad + k, n_rad) for k in range(n_rad)]

    barrier = pltpu.get_barrier_semaphore()
    pl.semaphore_signal(barrier, inc=1, device_id={"chan": partner}, device_id_type=MESH)
    for k in range(1, n_rad):
        pl.semaphore_signal(barrier, inc=1, device_id={"rad": rad_of[k]}, device_id_type=MESH)
    pl.semaphore_wait(barrier, n_rad)

    count_copies = []
    for k in range(1, n_rad):
        copy = pltpu.make_async_remote_copy(
            src_ref=count, dst_ref=counts.at[k], send_sem=k_send.at[k], recv_sem=k_recv.at[k],
            device_id={"rad": rad_of[k]}, device_id_type=MESH)
        copy.start()
        count_copies.append(copy)
    field_copies = {}
    for g in range(SLOTS):
        for x in range(2):
            part = (x, pl.ds(g * PTS, PTS))
            copy = pltpu.make_async_remote_copy(
                src_ref=v.at[part], dst_ref=other.at[part], send_sem=c_send.at[x, g],
                recv_sem=c_recv.at[x, g], device_id={"chan": partner}, device_id_type=MESH)
            copy.start()
            field_copies[x, g] = copy
    edge_copies = []
    for x in range(2):
        copy = pltpu.make_async_remote_copy(
            src_ref=v.at[x, 0], dst_ref=next_in.at[x], send_sem=e_send.at[x], recv_sem=e_recv.at[x],
            device_id={"rad": rad_of[n_rad - 1]}, device_id_type=MESH)
        copy.start()
        edge_copies.append(copy)

    k_high, k_low = kron_parts(kin_v[...], 16, 16, True)
    k_high, k_low = k_high[:, :PTS * 16], k_low[:, :PTS * 16]
    for g in range(SLOTS):
        for x in range(2):
            for cb in range(channels // 16):
                block = v[x, g * PTS:(g + 1) * PTS, cb * 16:(cb + 1) * 16, :].reshape(PTS * 16, width_two)
                res = mm(k_high, block) + mm(k_low, block)
                kin[x, g, :, cb * 16:(cb + 1) * 16, :] = res.reshape(16, 16, width_two)

    own_count = count[0:1, 0:1]
    two_slots = own_count >= 2
    for x in range(2):
        spill[x] = jnp.where(two_slots, kin[x, 1, PTS], kin[x, 0, PTS]).astype(jnp.bfloat16)
        copy = pltpu.make_async_remote_copy(
            src_ref=spill.at[x], dst_ref=below.at[x], send_sem=e_send.at[2 + x], recv_sem=e_recv.at[2 + x],
            device_id={"rad": rad_of[1]}, device_id_type=MESH)
        copy.start()
        edge_copies.append(copy)

    blocks = [(0, 8), (8, 7)]
    r_high, r_low = two_parts(rtwo[...])
    for g in range(SLOTS):
        for x in range(2):
            for p0, size in blocks:
                rows = pl.ds(g * PTS + p0, size)
                block = v[x, rows].reshape(size * channels, width_two)
                acc[x, rows] = (mm(block, r_high) + mm(block, r_low)).reshape(size, channels, width_two)
    own_high, own_low = kron_parts(m_own[...], 8, channels, False)
    oth_high, oth_low = kron_parts(m_oth[...], 8, channels, False)

    for copy in count_copies:
        copy.wait()
    offset = jnp.zeros((1, 1), jnp.int32)
    for k in range(1, n_rad):
        offset = offset + jnp.where(k <= me_rad, counts[k, 0:1, 0:1], 0)
    element = lax.broadcasted_iota(jnp.int32, widths.shape, 1)
    all_widths = widths[...]

    def width_at(index):
        found = jnp.sum(jnp.where(element == index, all_widths, 0.0), axis=1, keepdims=True)
        return jnp.where(found > 0.0, found, 1.0)

    r_two = inner_radius + radial_step * lax.broadcasted_iota(jnp.int32, (1, width_two), 1).astype(jnp.float32)
    inv_two = 1.0 / r_two
    first_l, second_l, mono = coef[:, 0:1], coef[:, 1:2], coef[:, 2:3]
    base = second_l * (inv_two * inv_two) - charge * inv_two

    for copy in edge_copies:
        copy.wait()
    inv_below = 1.0 / width_at(offset - 1)
    inv_below = jnp.where(me_rad > 0, inv_below * inv_below, 0.0)
    corner = kin_s[PTS, PTS]
    above = [jnp.where(me_rad < n_rad - 1, next_in[x].astype(jnp.float32), 0.0) for x in range(2)]
    inv_first = 1.0 / width_at(offset)
    inv_first = inv_first * inv_first
    for g in range(SLOTS):
        slot_width = width_at(offset + g)
        inv_w2 = 1.0 / slot_width
        inv_w2 = inv_w2 * inv_w2
        start = jnp.sum(jnp.where(element < offset + g, all_widths, 0.0), axis=1, keepdims=True)
        r_one = inner_radius + start + slot_width * fractions[:, 0:1]
        inv_one = 1.0 / r_one
        inv_far = 1.0 / jnp.maximum(r_one, r_two)
        weight = jnp.minimum(r_one, r_two) * inv_far * inv_far
        live = own_count > g
        for x in range(2):
            field_copies[x, g].wait()
            if g == 0:
                after = jnp.where(two_slots, v[x, PTS].astype(jnp.float32), above[x])
            else:
                after = above[x]
            after = after * inv_w2
            for p0, size in blocks:
                rows = pl.ds(g * PTS + p0, size)
                count_rows = size * channels
                mine = v[x, rows].reshape(count_rows, width_two)
                theirs = other[x, rows].reshape(count_rows, width_two)
                mix = mm(own_high[:count_rows, :count_rows], mine)
                mix = mix + mm(own_low[:count_rows, :count_rows], mine)
                mix = mix + mm(oth_high[:count_rows, :count_rows], theirs)
                mix = mix + mm(oth_low[:count_rows, :count_rows], theirs)
                for i in range(size):
                    q = p0 + i
                    row = g * PTS + q
                    mine_q = v[x, row].astype(jnp.float32)
                    potential = base + mono * inv_far[q:q + 1, :] + (
                        first_l * (inv_one[q:q + 1] * inv_one[q:q + 1]) - charge * inv_one[q:q + 1])
                    total = acc[x, row] + kin[x, g, q] * inv_w2 + kin_s[q, PTS] * after
                    total = total + potential * mine_q
                    total = total + weight[q:q + 1, :] * mix[i * channels:(i + 1) * channels]
                    if q == 0:
                        if g == 0:
                            total = total + (below[x].astype(jnp.float32) + corner * mine_q) * inv_below
                        else:
                            total = total + (kin[x, 0, PTS] + corner * mine_q) * inv_first
                    step = time_step if x == 1 else -time_step
                    result = v[1 - x, row].astype(jnp.float32) + step * total
                    out[1 - x, row] = jnp.where(live, result, 0.0)


def per_device(n_rad, wave, tile_elems, element_width, element_kinetic, radial_two, angular, channel_table):
    channels, _, rows, width_two = wave.shape
    field = wave.transpose(1, 2, 0, 3)
    count = jnp.broadcast_to(tile_elems[:, None], (8, 128))
    total = element_width.shape[0]
    lanes = -(-total // 128) * 128
    widths = jnp.pad(element_width, (0, lanes - total))[None, :]
    fractions = 0.5 * (1.0 - jnp.cos(jnp.pi * jnp.arange(16, dtype=jnp.float32) / PTS))
    fractions = jnp.broadcast_to(fractions[:, None], (16, 128))
    me = lax.axis_index("chan")
    own = lax.dynamic_slice_in_dim(channel_table, me * channels, channels, 0)
    oth = lax.dynamic_slice_in_dim(channel_table, (1 - me) * channels, channels, 0)

    def allowed(a, b):
        low = jnp.abs(a[:, None] - b[None, :])
        high = a[:, None] + b[None, :]
        return (low <= 1) & (1 <= high) & ((high + 1) % 2 == 0)

    def coupling(cols, first):
        keep = allowed(own[:, 0], cols[:, 0]) & allowed(own[:, 1], cols[:, 1])
        there = lax.dynamic_slice(angular[1], (me * channels, first), (channels, channels))
        back = lax.dynamic_slice(angular[1], (first, me * channels), (channels, channels))
        return jnp.where(keep, 0.5 * (there + back.T), 0.0)

    m_own = coupling(own, me * channels)
    m_oth = coupling(oth, (1 - me) * channels)
    block = lax.dynamic_slice(angular[0], (me * channels, me * channels), (channels, channels))
    mono = jnp.sum(jnp.where(jnp.eye(channels, dtype=bool), block, 0.0), axis=1)
    orbital = own.astype(jnp.float32)
    centri = 0.5 * orbital * (orbital + 1.0)
    coef = jnp.concatenate([centri, mono[:, None]], axis=1)

    vmem = pl.BlockSpec(memory_space=pltpu.VMEM)
    smem = pl.BlockSpec(memory_space=pltpu.SMEM)
    moved = pl.pallas_call(
        functools.partial(kernel, n_rad),
        out_shape=jax.ShapeDtypeStruct((2, rows, channels, width_two), jnp.float32),
        in_specs=[vmem, vmem, vmem, vmem, smem, vmem, vmem, vmem, vmem, vmem],
        out_specs=vmem,
        scratch_shapes=[
            pltpu.VMEM((2, rows, channels, width_two), jnp.bfloat16),
            pltpu.VMEM((2, channels, width_two), jnp.bfloat16),
            pltpu.VMEM((2, channels, width_two), jnp.bfloat16),
            pltpu.VMEM((2, channels, width_two), jnp.bfloat16),
            pltpu.VMEM((n_rad, 8, 128), jnp.int32),
            pltpu.VMEM((2, SLOTS, 16, channels, width_two), jnp.float32),
            pltpu.VMEM((2, rows, channels, width_two), jnp.float32),
            pltpu.SemaphoreType.DMA((2, SLOTS)),
            pltpu.SemaphoreType.DMA((2, SLOTS)),
            pltpu.SemaphoreType.DMA((n_rad,)),
            pltpu.SemaphoreType.DMA((n_rad,)),
            pltpu.SemaphoreType.DMA((4,)),
            pltpu.SemaphoreType.DMA((4,)),
        ],
        compiler_params=pltpu.CompilerParams(
            collective_id=0, has_side_effects=True, vmem_limit_bytes=44 * 1024 * 1024),
        cost_estimate=pl.CostEstimate(flops=6_000_000_000, bytes_accessed=10_000_000, transcendentals=0),
    )(field, count, widths, fractions, element_kinetic, element_kinetic, radial_two, m_own, m_oth, coef)
    return moved.transpose(2, 0, 1, 3)


def solution(mesh):
    in_specs = (P("chan", None, "rad", "grp"), P(("grp", "rad")), P("grp"), P(), P(), P(), P())
    out_specs = P("chan", None, "rad", "grp")
    return jax.shard_map(
        functools.partial(per_device, mesh.shape["rad"]), mesh=mesh, in_specs=in_specs,
        out_specs=out_specs, check_vma=False)
```

```python
import functools
import math

import jax
import jax.numpy as jnp
from jax import lax
from jax.experimental import pallas as pl
from jax.experimental.pallas import tpu as pltpu
from jax.sharding import PartitionSpec as P

PTS = 15
SLOTS = 2
MESH = pl.DeviceIdType.MESH
highest = lax.Precision.HIGHEST
charge = 2.0
inner_radius = 4.0
radial_step = 0.1
time_step = 0.1


def mm(a, b):
    return jnp.dot(a, b, preferred_element_type=jnp.float32)


def two_parts(a):
    high = a.astype(jnp.bfloat16)
    return high, (a - high.astype(jnp.float32)).astype(jnp.bfloat16)


def one_hot(shape, index):
    return (index == lax.broadcasted_iota(jnp.int32, shape, 1)).astype(jnp.float32)


def rows_of(shape):
    return lax.broadcasted_iota(jnp.int32, shape, 0)


def cols_of(shape):
    return lax.broadcasted_iota(jnp.int32, shape, 1)


def spread(pick_rows, matrix, pick_cols):
    first = jnp.dot(pick_rows, matrix, precision=highest, preferred_element_type=jnp.float32)
    return lax.dot_general(
        first, pick_cols, (((1,), (1,)), ((), ())), precision=highest, preferred_element_type=jnp.float32)


def kinetic_parts(kinetic):
    pick = one_hot((256, 16), rows_of((256, 16)) // 16)
    keep = rows_of((256, 256)) % 16 == cols_of((256, 256)) % 16
    return two_parts(jnp.where(keep, spread(pick, kinetic, pick), 0.0))


def channel_parts(table, angular, me, channels, points):
    every = 2 * channels
    square = (every, every)
    eye = rows_of(square) == cols_of(square)
    keep = None
    for electron in range(2):
        row = table[electron:electron + 1, :].astype(jnp.float32)
        column = jnp.sum(jnp.where(eye, row, 0.0), axis=1, keepdims=True)
        apart = jnp.abs(column - row) == 1.0
        keep = apart if keep is None else keep & apart
    turned = lax.dot_general(
        eye.astype(jnp.float32), angular[1], (((1,), (1,)), ((), ())), precision=highest,
        preferred_element_type=jnp.float32)
    matrix = jnp.where(keep, 0.5 * (angular[1] + turned), 0.0)
    out_rows, in_rows = points * channels, points * every
    pick_r = one_hot((out_rows, every), me * channels + rows_of((out_rows, every)) % channels)
    pick_c = one_hot((in_rows, every), (rows_of((in_rows, every)) + me * channels) % every)
    same = rows_of((out_rows, in_rows)) // channels == cols_of((out_rows, in_rows)) // every
    return two_parts(jnp.where(same, spread(pick_r, matrix, pick_c), 0.0))


def own_columns(table, angular, me, channels):
    shape = (channels, 2 * channels)
    mine = rows_of(shape) + me * channels == cols_of(shape)

    def column(row):
        return jnp.sum(jnp.where(mine, row, 0.0), axis=1, keepdims=True)

    first = column(table[0:1, :].astype(jnp.float32))
    second = column(table[1:2, :].astype(jnp.float32))
    square = (2 * channels, 2 * channels)
    diagonal = jnp.where(rows_of(square) == cols_of(square), angular[0], 0.0)
    mono = column(jnp.sum(diagonal, axis=0, keepdims=True))
    return 0.5 * first * (first + 1.0), 0.5 * second * (second + 1.0), mono


def kernel(
    n_rad, raw, tile_elems, widths, kin_s, kin_v, rtwo, angular, table, out,
    full, next_in, below, spill, count, counts, kin, acc,
    c_send, c_recv, k_send, k_recv, e_send, e_recv,
):
    local_rows, channels, width_two = acc.shape[1:]
    lane_tiles = width_two // 128
    pitch = local_rows * lane_tiles * 2
    me_rad = lax.axis_index("rad")
    me_chan = lax.axis_index("chan")
    partner = 1 - me_chan
    rad_of = [lax.rem(me_rad + k, n_rad) for k in range(n_rad)]

    def place(x, row, tile):
        return pl.ds((row * lane_tiles + tile) * 2 + x, channels, stride=pitch)

    barrier = pltpu.get_barrier_semaphore()
    pl.semaphore_signal(barrier, inc=1, device_id={"chan": partner}, device_id_type=MESH)
    for k in range(1, n_rad):
        pl.semaphore_signal(barrier, inc=1, device_id={"rad": rad_of[k]}, device_id_type=MESH)
    count[...] = jnp.full(count.shape, tile_elems[0], jnp.int32)

    for c in range(0, channels, 4):
        out[c * pitch:(c + 4) * pitch, :] = raw[c * pitch:(c + 4) * pitch, :].astype(jnp.float32)

    def unpack(g):
        for row in range(g * PTS, (g + 1) * PTS):
            for x in range(2):
                for tile in range(lane_tiles):
                    full[x, row, 0:channels, tile * 128:(tile + 1) * 128] = out[
                        place(x, row, tile), :].astype(jnp.bfloat16)

    unpack(0)
    pl.semaphore_wait(barrier, n_rad)
    count_copies = []
    for k in range(1, n_rad):
        copy = pltpu.make_async_remote_copy(
            src_ref=count, dst_ref=counts.at[k], send_sem=k_send.at[k], recv_sem=k_recv.at[k],
            device_id={"rad": rad_of[k]}, device_id_type=MESH)
        copy.start()
        count_copies.append(copy)
    edge_copies = []
    for x in range(2):
        copy = pltpu.make_async_remote_copy(
            src_ref=full.at[x, 0, pl.ds(0, channels)], dst_ref=next_in.at[x], send_sem=e_send.at[x],
            recv_sem=e_recv.at[x], device_id={"rad": rad_of[n_rad - 1]}, device_id_type=MESH)
        copy.start()
        edge_copies.append(copy)
    field_copies = {}
    for g in range(SLOTS):
        if g > 0:
            unpack(g)
        for x in range(2):
            copy = pltpu.make_async_remote_copy(
                src_ref=full.at[x, pl.ds(g * PTS, PTS), pl.ds(0, channels)],
                dst_ref=full.at[x, pl.ds(g * PTS, PTS), pl.ds(channels, channels)],
                send_sem=c_send.at[x, g], recv_sem=c_recv.at[x, g],
                device_id={"chan": partner}, device_id_type=MESH)
            copy.start()
            field_copies[x, g] = copy

    k_high, k_low = kinetic_parts(kin_v[...])
    k_high, k_low = k_high[:, :PTS * 16], k_low[:, :PTS * 16]
    for g in range(SLOTS):
        for x in range(2):
            for cb in range(channels // 16):
                block = full[x, g * PTS:(g + 1) * PTS, cb * 16:(cb + 1) * 16, :].reshape(PTS * 16, width_two)
                res = mm(k_high, block) + mm(k_low, block)
                kin[x, g, :, cb * 16:(cb + 1) * 16, :] = res.reshape(16, 16, width_two)

    own_count = count[0:1, 0:1]
    two_slots = own_count >= 2
    for x in range(2):
        spill[x] = jnp.where(two_slots, kin[x, 1, PTS], kin[x, 0, PTS]).astype(jnp.bfloat16)
        copy = pltpu.make_async_remote_copy(
            src_ref=spill.at[x], dst_ref=below.at[x], send_sem=e_send.at[2 + x], recv_sem=e_recv.at[2 + x],
            device_id={"rad": rad_of[1]}, device_id_type=MESH)
        copy.start()
        edge_copies.append(copy)

    r_high, r_low = two_parts(rtwo[...])
    for g in range(SLOTS):
        for x in range(2):
            for p0, size in ((0, 8), (8, 7)):
                rows = pl.ds(g * PTS + p0, size)
                block = full[x, rows, 0:channels, :].reshape(size * channels, width_two)
                acc[x, rows] = (mm(block, r_high) + mm(block, r_low)).reshape(size, channels, width_two)
    m_high, m_low = channel_parts(table, angular, me_chan, channels, 4)
    first_l, second_l, mono = own_columns(table, angular, me_chan, channels)

    for copy in count_copies:
        copy.wait()
    offset = jnp.zeros((1, 1), jnp.int32)
    for k in range(1, n_rad):
        offset = offset + jnp.where(k <= me_rad, counts[k, 0:1, 0:1], 0)
    element = cols_of(widths.shape)
    all_widths = widths[...]

    def width_at(index):
        found = jnp.sum(jnp.where(element == index, all_widths, 0.0), axis=1, keepdims=True)
        return jnp.where(found > 0.0, found, 1.0)

    r_two = inner_radius + radial_step * cols_of((1, width_two)).astype(jnp.float32)
    inv_two = 1.0 / r_two
    base = second_l * (inv_two * inv_two) - charge * inv_two
    point = rows_of((16, 1))
    fractions = jnp.zeros((16, 1), jnp.float32)
    for p in range(1, 16):
        fractions = jnp.where(point == p, 0.5 * (1.0 - math.cos(math.pi * p / PTS)), fractions)

    for copy in edge_copies:
        copy.wait()
    inv_below = 1.0 / width_at(offset - 1)
    inv_below = jnp.where(me_rad > 0, inv_below * inv_below, 0.0)
    corner = kin_s[PTS, PTS]
    above = [jnp.where(me_rad < n_rad - 1, next_in[x].astype(jnp.float32), 0.0) for x in range(2)]
    inv_first = 1.0 / width_at(offset)
    inv_first = inv_first * inv_first
    for g in range(SLOTS):
        slot_width = width_at(offset + g)
        inv_w2 = 1.0 / slot_width
        inv_w2 = inv_w2 * inv_w2
        start = jnp.sum(jnp.where(element < offset + g, all_widths, 0.0), axis=1, keepdims=True)
        r_one = inner_radius + start + slot_width * fractions
        inv_one = 1.0 / r_one
        inv_far = 1.0 / jnp.maximum(r_one, r_two)
        weight = jnp.minimum(r_one, r_two) * inv_far * inv_far
        live = own_count > g
        for x in range(2):
            field_copies[x, g].wait()
            if g == 0:
                after = jnp.where(two_slots, full[x, PTS, 0:channels, :].astype(jnp.float32), above[x])
            else:
                after = above[x]
            after = after * inv_w2
            for p0, size in ((0, 4), (4, 4), (8, 4), (12, 3)):
                block = full[x, pl.ds(g * PTS + p0, size)].reshape(size * 2 * channels, width_two)
                used = (slice(0, size * channels), slice(0, size * 2 * channels))
                mix = mm(m_high[used], block) + mm(m_low[used], block)
                for i in range(size):
                    q = p0 + i
                    row = g * PTS + q
                    mine_q = full[x, row, 0:channels, :].astype(jnp.float32)
                    potential = base + mono * inv_far[q:q + 1, :] + (
                        first_l * (inv_one[q:q + 1] * inv_one[q:q + 1]) - charge * inv_one[q:q + 1])
                    total = acc[x, row] + kin[x, g, q] * inv_w2 + kin_s[q, PTS] * after
                    total = total + potential * mine_q
                    total = total + weight[q:q + 1, :] * mix[i * channels:(i + 1) * channels]
                    if q == 0:
                        if g == 0:
                            total = total + (below[x].astype(jnp.float32) + corner * mine_q) * inv_below
                        else:
                            total = total + (kin[x, 0, PTS] + corner * mine_q) * inv_first
                    step = time_step if x == 1 else -time_step
                    result = full[1 - x, row, 0:channels, :].astype(jnp.float32) + step * total
                    result = jnp.where(live, result, 0.0)
                    for tile in range(lane_tiles):
                        out[place(1 - x, row, tile), :] = result[:, tile * 128:(tile + 1) * 128]


def per_device(n_rad, wave, tile_elems, element_width, element_kinetic, radial_two, angular, channel_table):
    channels, _, rows, width_two = wave.shape
    tiles = width_two // 128
    raw = wave.reshape(channels, 2, rows, tiles, 128).transpose(0, 2, 3, 1, 4).reshape(-1, 128)
    vmem = pl.BlockSpec(memory_space=pltpu.VMEM)
    smem = pl.BlockSpec(memory_space=pltpu.SMEM)
    edge = pltpu.VMEM((2, channels, width_two), jnp.bfloat16)
    evolved = pl.pallas_call(
        functools.partial(kernel, n_rad),
        out_shape=jax.ShapeDtypeStruct(raw.shape, jnp.float32),
        in_specs=[vmem, smem, vmem, smem, vmem, vmem, vmem, vmem],
        out_specs=vmem,
        scratch_shapes=[
            pltpu.VMEM((2, rows, 2 * channels, width_two), jnp.bfloat16),
            edge, edge, edge,
            pltpu.VMEM((8, 128), jnp.int32),
            pltpu.VMEM((n_rad, 8, 128), jnp.int32),
            pltpu.VMEM((2, SLOTS, 16, channels, width_two), jnp.float32),
            pltpu.VMEM((2, rows, channels, width_two), jnp.float32),
            pltpu.SemaphoreType.DMA((2, SLOTS)),
            pltpu.SemaphoreType.DMA((2, SLOTS)),
            pltpu.SemaphoreType.DMA((n_rad,)),
            pltpu.SemaphoreType.DMA((n_rad,)),
            pltpu.SemaphoreType.DMA((4,)),
            pltpu.SemaphoreType.DMA((4,)),
        ],
        compiler_params=pltpu.CompilerParams(
            collective_id=0, has_side_effects=True, vmem_limit_bytes=44 * 1024 * 1024),
        cost_estimate=pl.CostEstimate(flops=6_000_000_000, bytes_accessed=10_000_000, transcendentals=0),
    )(raw, tile_elems, element_width[None, :], element_kinetic, element_kinetic, radial_two, angular,
      channel_table.T)
    evolved = evolved.reshape(channels, rows, tiles, 2, 128).transpose(0, 3, 1, 2, 4)
    return evolved.reshape(wave.shape)


def solution(mesh):
    in_specs = (P("chan", None, "rad", "grp"), P(("grp", "rad")), P("grp"), P(), P(), P(), P())
    out_specs = P("chan", None, "rad", "grp")
    return jax.shard_map(
        functools.partial(per_device, mesh.shape["rad"]), mesh=mesh, in_specs=in_specs,
        out_specs=out_specs, check_vma=False)
```

```python
import functools
import math

import jax
import jax.numpy as jnp
from jax import lax
from jax.experimental import pallas as pl
from jax.experimental.pallas import tpu as pltpu
from jax.sharding import PartitionSpec as P

PTS = 15
SLOTS = 2
RAW_HEAD = 128
MESH = pl.DeviceIdType.MESH
highest = lax.Precision.HIGHEST
charge = 2.0
inner_radius = 4.0
radial_step = 0.1
time_step = 0.1


def mm(a, b):
    return jnp.dot(a, b, preferred_element_type=jnp.float32)


def two_parts(a):
    high = a.astype(jnp.bfloat16)
    return high, (a - high.astype(jnp.float32)).astype(jnp.bfloat16)


def one_hot(shape, index):
    return (index == lax.broadcasted_iota(jnp.int32, shape, 1)).astype(jnp.float32)


def rows_of(shape):
    return lax.broadcasted_iota(jnp.int32, shape, 0)


def cols_of(shape):
    return lax.broadcasted_iota(jnp.int32, shape, 1)


def spread(pick_rows, matrix, pick_cols):
    first = jnp.dot(pick_rows, matrix, precision=highest, preferred_element_type=jnp.float32)
    return lax.dot_general(
        first, pick_cols, (((1,), (1,)), ((), ())), precision=highest, preferred_element_type=jnp.float32)


def kinetic_parts(kinetic):
    pick = one_hot((256, 16), rows_of((256, 16)) // 16)
    keep = rows_of((256, 256)) % 16 == cols_of((256, 256)) % 16
    return two_parts(jnp.where(keep, spread(pick, kinetic, pick), 0.0))


def channel_parts(table, angular, me, channels, points):
    every = 2 * channels
    square = (every, every)
    eye = rows_of(square) == cols_of(square)
    keep = None
    for electron in range(2):
        row = table[electron:electron + 1, :].astype(jnp.float32)
        column = jnp.sum(jnp.where(eye, row, 0.0), axis=1, keepdims=True)
        apart = jnp.abs(column - row) == 1.0
        keep = apart if keep is None else keep & apart
    turned = lax.dot_general(
        eye.astype(jnp.float32), angular[1], (((1,), (1,)), ((), ())), precision=highest,
        preferred_element_type=jnp.float32)
    matrix = jnp.where(keep, 0.5 * (angular[1] + turned), 0.0)
    out_rows, in_rows = points * channels, points * every
    pick_r = one_hot((out_rows, every), me * channels + rows_of((out_rows, every)) % channels)
    pick_c = one_hot((in_rows, every), (rows_of((in_rows, every)) + me * channels) % every)
    same = rows_of((out_rows, in_rows)) // channels == cols_of((out_rows, in_rows)) // every
    return two_parts(jnp.where(same, spread(pick_r, matrix, pick_c), 0.0))


def own_columns(table, angular, me, channels):
    shape = (channels, 2 * channels)
    mine = rows_of(shape) + me * channels == cols_of(shape)

    def column(row):
        return jnp.sum(jnp.where(mine, row, 0.0), axis=1, keepdims=True)

    first = column(table[0:1, :].astype(jnp.float32))
    second = column(table[1:2, :].astype(jnp.float32))
    square = (2 * channels, 2 * channels)
    diagonal = jnp.where(rows_of(square) == cols_of(square), angular[0], 0.0)
    mono = column(jnp.sum(diagonal, axis=0, keepdims=True))
    return 0.5 * first * (first + 1.0), 0.5 * second * (second + 1.0), mono


def kernel(
    n_rad, raw_hbm, tile_elems, widths_hbm, kin_hbm, rtwo_hbm, angular_hbm, table_hbm, out_hbm,
    out, o_sem, raw, widths, kin_v, rtwo, angular, table, l_sem, full, next_in, below, spill, count, counts, kin, acc,
    c_send, c_recv, k_send, k_recv, e_send, e_recv,
):
    local_rows, channels, width_two = acc.shape[1:]
    lane_tiles = width_two // 128
    pitch = local_rows * lane_tiles * 2
    me_rad = lax.axis_index("rad")
    me_chan = lax.axis_index("chan")
    partner = 1 - me_chan
    rad_of = [lax.rem(me_rad + k, n_rad) for k in range(n_rad)]

    def place(x, row, tile):
        return pl.ds((row * lane_tiles + tile) * 2 + x, channels, stride=pitch)

    loads = []
    for source, target in (
        (raw_hbm.at[:, pl.ds(0, RAW_HEAD)], raw.at[:, pl.ds(0, RAW_HEAD)]),
        (raw_hbm.at[:, pl.ds(RAW_HEAD, pitch - RAW_HEAD)], raw.at[:, pl.ds(RAW_HEAD, pitch - RAW_HEAD)]),
        (kin_hbm, kin_v), (rtwo_hbm, rtwo), (angular_hbm, angular), (table_hbm, table), (widths_hbm, widths),
    ):
        load = pltpu.make_async_copy(source, target, l_sem.at[len(loads)])
        load.start()
        loads.append(load)
    barrier = pltpu.get_barrier_semaphore()
    pl.semaphore_signal(barrier, inc=1, device_id={"chan": partner}, device_id_type=MESH)
    for k in range(1, n_rad):
        pl.semaphore_signal(barrier, inc=1, device_id={"rad": rad_of[k]}, device_id_type=MESH)
    count[...] = jnp.full(count.shape, tile_elems[0], jnp.int32)

    def widen(begin, end):
        for c in range(channels):
            out[c * pitch + begin:c * pitch + end, :] = raw[c, begin:end, :].astype(jnp.float32)

    def unpack(g):
        for row in range(g * PTS, (g + 1) * PTS):
            for x in range(2):
                for tile in range(lane_tiles):
                    full[x, row, 0:channels, tile * 128:(tile + 1) * 128] = out[
                        place(x, row, tile), :].astype(jnp.bfloat16)

    loads[0].wait()
    widen(0, RAW_HEAD)
    unpack(0)
    pl.semaphore_wait(barrier, n_rad)
    count_copies = []
    for k in range(1, n_rad):
        copy = pltpu.make_async_remote_copy(
            src_ref=count, dst_ref=counts.at[k], send_sem=k_send.at[k], recv_sem=k_recv.at[k],
            device_id={"rad": rad_of[k]}, device_id_type=MESH)
        copy.start()
        count_copies.append(copy)
    edge_copies = []
    for x in range(2):
        copy = pltpu.make_async_remote_copy(
            src_ref=full.at[x, 0, pl.ds(0, channels)], dst_ref=next_in.at[x], send_sem=e_send.at[x],
            recv_sem=e_recv.at[x], device_id={"rad": rad_of[n_rad - 1]}, device_id_type=MESH)
        copy.start()
        edge_copies.append(copy)
    field_copies = {}
    for g in range(SLOTS):
        if g > 0:
            loads[1].wait()
            widen(RAW_HEAD, pitch)
            unpack(g)
        for x in range(2):
            copy = pltpu.make_async_remote_copy(
                src_ref=full.at[x, pl.ds(g * PTS, PTS), pl.ds(0, channels)],
                dst_ref=full.at[x, pl.ds(g * PTS, PTS), pl.ds(channels, channels)],
                send_sem=c_send.at[x, g], recv_sem=c_recv.at[x, g],
                device_id={"chan": partner}, device_id_type=MESH)
            copy.start()
            field_copies[x, g] = copy

    loads[2].wait()
    k_high, k_low = kinetic_parts(kin_v[...])
    k_high, k_low = k_high[:, :PTS * 16], k_low[:, :PTS * 16]
    for g in range(SLOTS):
        for x in range(2):
            for cb in range(channels // 16):
                block = full[x, g * PTS:(g + 1) * PTS, cb * 16:(cb + 1) * 16, :].reshape(PTS * 16, width_two)
                res = mm(k_high, block) + mm(k_low, block)
                kin[x, g, :, cb * 16:(cb + 1) * 16, :] = res.reshape(16, 16, width_two)

    own_count = count[0:1, 0:1]
    two_slots = own_count >= 2
    for x in range(2):
        spill[x] = jnp.where(two_slots, kin[x, 1, PTS], kin[x, 0, PTS]).astype(jnp.bfloat16)
        copy = pltpu.make_async_remote_copy(
            src_ref=spill.at[x], dst_ref=below.at[x], send_sem=e_send.at[2 + x], recv_sem=e_recv.at[2 + x],
            device_id={"rad": rad_of[1]}, device_id_type=MESH)
        copy.start()
        edge_copies.append(copy)

    loads[3].wait()
    r_high, r_low = two_parts(rtwo[...])
    for g in range(SLOTS):
        for x in range(2):
            for p0, size in ((0, 8), (8, 7)):
                rows = pl.ds(g * PTS + p0, size)
                block = full[x, rows, 0:channels, :].reshape(size * channels, width_two)
                acc[x, rows] = (mm(block, r_high) + mm(block, r_low)).reshape(size, channels, width_two)
    for load in loads[4:]:
        load.wait()
    m_high, m_low = channel_parts(table, angular, me_chan, channels, 4)
    first_l, second_l, mono = own_columns(table, angular, me_chan, channels)

    for copy in count_copies:
        copy.wait()
    offset = jnp.zeros((1, 1), jnp.int32)
    for k in range(1, n_rad):
        offset = offset + jnp.where(k <= me_rad, counts[k, 0:1, 0:1], 0)
    element = cols_of(widths.shape)
    all_widths = widths[...]

    def width_at(index):
        found = jnp.sum(jnp.where(element == index, all_widths, 0.0), axis=1, keepdims=True)
        return jnp.where(found > 0.0, found, 1.0)

    r_two = inner_radius + radial_step * cols_of((1, width_two)).astype(jnp.float32)
    inv_two = 1.0 / r_two
    base = second_l * (inv_two * inv_two) - charge * inv_two
    point = rows_of((16, 1))
    fractions = jnp.zeros((16, 1), jnp.float32)
    for p in range(1, 16):
        fractions = jnp.where(point == p, 0.5 * (1.0 - math.cos(math.pi * p / PTS)), fractions)

    for copy in edge_copies:
        copy.wait()
    inv_below = 1.0 / width_at(offset - 1)
    inv_below = jnp.where(me_rad > 0, inv_below * inv_below, 0.0)
    corner = kin_v[PTS:PTS + 1, PTS:PTS + 1]
    above = [jnp.where(me_rad < n_rad - 1, next_in[x].astype(jnp.float32), 0.0) for x in range(2)]
    inv_first = 1.0 / width_at(offset)
    inv_first = inv_first * inv_first
    stores = []
    for g in range(SLOTS):
        slot_width = width_at(offset + g)
        inv_w2 = 1.0 / slot_width
        inv_w2 = inv_w2 * inv_w2
        start = jnp.sum(jnp.where(element < offset + g, all_widths, 0.0), axis=1, keepdims=True)
        r_one = inner_radius + start + slot_width * fractions
        inv_one = 1.0 / r_one
        inv_far = 1.0 / jnp.maximum(r_one, r_two)
        weight = jnp.minimum(r_one, r_two) * inv_far * inv_far
        live = own_count > g
        after = []
        for x in range(2):
            field_copies[x, g].wait()
            if g == 0:
                row = jnp.where(two_slots, full[x, PTS, 0:channels, :].astype(jnp.float32), above[x])
            else:
                row = above[x]
            after.append(row * inv_w2)
        for part, (p0, size) in enumerate(((0, 4), (4, 4), (8, 4), (12, 3))):
            used = (slice(0, size * channels), slice(0, size * 2 * channels))
            for x in range(2):
                block = full[x, pl.ds(g * PTS + p0, size)].reshape(size * 2 * channels, width_two)
                mix = mm(m_high[used], block) + mm(m_low[used], block)
                for i in range(size):
                    q = p0 + i
                    row = g * PTS + q
                    mine_q = full[x, row, 0:channels, :].astype(jnp.float32)
                    potential = base + mono * inv_far[q:q + 1, :] + (
                        first_l * (inv_one[q:q + 1] * inv_one[q:q + 1]) - charge * inv_one[q:q + 1])
                    total = acc[x, row] + kin[x, g, q] * inv_w2 + kin_v[q:q + 1, PTS:PTS + 1] * after[x]
                    total = total + potential * mine_q
                    total = total + weight[q:q + 1, :] * mix[i * channels:(i + 1) * channels]
                    if q == 0:
                        if g == 0:
                            total = total + (below[x].astype(jnp.float32) + corner * mine_q) * inv_below
                        else:
                            total = total + (kin[x, 0, PTS] + corner * mine_q) * inv_first
                    step = time_step if x == 1 else -time_step
                    result = full[1 - x, row, 0:channels, :].astype(jnp.float32) + step * total
                    result = jnp.where(live, result, 0.0)
                    for tile in range(lane_tiles):
                        out[place(1 - x, row, tile), :] = result[:, tile * 128:(tile + 1) * 128]
            span = pl.ds((g * PTS + p0) * lane_tiles * 2, size * lane_tiles * 2)
            store = pltpu.make_async_copy(
                out.reshape(channels, pitch, 128).at[:, span], out_hbm.at[:, span], o_sem.at[g, part])
            store.start()
            stores.append(store)
    for store in stores:
        store.wait()


def per_device(n_rad, wave, tile_elems, element_width, element_kinetic, radial_two, angular, channel_table):
    channels, _, rows, width_two = wave.shape
    tiles = width_two // 128
    raw = wave.reshape(channels, 2, rows, tiles, 128).transpose(0, 2, 3, 1, 4)
    raw = raw.reshape(channels, -1, 128)
    hbm = pl.BlockSpec(memory_space=pltpu.HBM)
    smem = pl.BlockSpec(memory_space=pltpu.SMEM)
    edge = pltpu.VMEM((2, channels, width_two), jnp.bfloat16)
    evolved = pl.pallas_call(
        functools.partial(kernel, n_rad),
        out_shape=jax.ShapeDtypeStruct(raw.shape, jnp.float32),
        in_specs=[hbm, smem, hbm, hbm, hbm, hbm, hbm],
        out_specs=hbm,
        scratch_shapes=[
            pltpu.VMEM((raw.shape[0] * raw.shape[1], 128), jnp.float32),
            pltpu.SemaphoreType.DMA((SLOTS, 4)),
            pltpu.VMEM(raw.shape, jnp.bfloat16),
            pltpu.VMEM((1, element_width.shape[0]), jnp.float32),
            pltpu.VMEM(element_kinetic.shape, jnp.float32),
            pltpu.VMEM(radial_two.shape, jnp.float32),
            pltpu.VMEM(angular.shape, jnp.float32),
            pltpu.VMEM(channel_table.shape[::-1], jnp.int32),
            pltpu.SemaphoreType.DMA((7,)),
            pltpu.VMEM((2, rows, 2 * channels, width_two), jnp.bfloat16),
            edge, edge, edge,
            pltpu.VMEM((8, 128), jnp.int32),
            pltpu.VMEM((n_rad, 8, 128), jnp.int32),
            pltpu.VMEM((2, SLOTS, 16, channels, width_two), jnp.float32),
            pltpu.VMEM((2, rows, channels, width_two), jnp.float32),
            pltpu.SemaphoreType.DMA((2, SLOTS)),
            pltpu.SemaphoreType.DMA((2, SLOTS)),
            pltpu.SemaphoreType.DMA((n_rad,)),
            pltpu.SemaphoreType.DMA((n_rad,)),
            pltpu.SemaphoreType.DMA((4,)),
            pltpu.SemaphoreType.DMA((4,)),
        ],
        compiler_params=pltpu.CompilerParams(
            collective_id=0, has_side_effects=True, vmem_limit_bytes=62 * 1024 * 1024),
        cost_estimate=pl.CostEstimate(flops=6_000_000_000, bytes_accessed=10_000_000, transcendentals=0),
    )(raw, tile_elems, element_width[None, :], element_kinetic, radial_two, angular,
      channel_table.T)
    evolved = evolved.reshape(channels, rows, tiles, 2, 128).transpose(0, 3, 1, 2, 4)
    return evolved.reshape(wave.shape)


def solution(mesh):
    in_specs = (P("chan", None, "rad", "grp"), P(("grp", "rad")), P("grp"), P(), P(), P(), P())
    out_specs = P("chan", None, "rad", "grp")
    return jax.shard_map(
        functools.partial(per_device, mesh.shape["rad"]), mesh=mesh, in_specs=in_specs,
        out_specs=out_specs, check_vma=False)
```

```python
import functools
import math

import jax
import jax.numpy as jnp
from jax import lax
from jax.experimental import pallas as pl
from jax.experimental.pallas import tpu as pltpu
from jax.sharding import PartitionSpec as P

PTS = 15
SLOTS = 2
RAW_HEAD = 128
MESH = pl.DeviceIdType.MESH
highest = lax.Precision.HIGHEST
charge = 2.0
inner_radius = 4.0
radial_step = 0.1
time_step = 0.1


def mm(a, b):
    return jnp.dot(a, b, preferred_element_type=jnp.float32)


def two_parts(a):
    high = a.astype(jnp.bfloat16)
    return high, (a - high.astype(jnp.float32)).astype(jnp.bfloat16)


def one_hot(shape, index):
    return (index == lax.broadcasted_iota(jnp.int32, shape, 1)).astype(jnp.float32)


def rows_of(shape):
    return lax.broadcasted_iota(jnp.int32, shape, 0)


def cols_of(shape):
    return lax.broadcasted_iota(jnp.int32, shape, 1)


def spread(pick_rows, matrix, pick_cols):
    first = jnp.dot(pick_rows, matrix, precision=highest, preferred_element_type=jnp.float32)
    return lax.dot_general(
        first, pick_cols, (((1,), (1,)), ((), ())), precision=highest, preferred_element_type=jnp.float32)


def kinetic_parts(kinetic):
    pick = one_hot((256, 16), rows_of((256, 16)) // 16)
    keep = rows_of((256, 256)) % 16 == cols_of((256, 256)) % 16
    return two_parts(jnp.where(keep, spread(pick, kinetic, pick), 0.0))


def channel_parts(table, angular, me, channels, points):
    every = 2 * channels
    square = (every, every)
    eye = rows_of(square) == cols_of(square)
    keep = None
    for electron in range(2):
        row = table[electron:electron + 1, :].astype(jnp.float32)
        column = jnp.sum(jnp.where(eye, row, 0.0), axis=1, keepdims=True)
        apart = jnp.abs(column - row) == 1.0
        keep = apart if keep is None else keep & apart
    turned = lax.dot_general(
        eye.astype(jnp.float32), angular[1], (((1,), (1,)), ((), ())), precision=highest,
        preferred_element_type=jnp.float32)
    matrix = jnp.where(keep, 0.5 * (angular[1] + turned), 0.0)
    out_rows, in_rows = points * channels, points * every
    pick_r = one_hot((out_rows, every), me * channels + rows_of((out_rows, every)) % channels)
    pick_c = one_hot((in_rows, every), (rows_of((in_rows, every)) + me * channels) % every)
    same = rows_of((out_rows, in_rows)) // channels == cols_of((out_rows, in_rows)) // every
    return two_parts(jnp.where(same, spread(pick_r, matrix, pick_c), 0.0))


def own_columns(table, angular, me, channels):
    shape = (channels, 2 * channels)
    mine = rows_of(shape) + me * channels == cols_of(shape)

    def column(row):
        return jnp.sum(jnp.where(mine, row, 0.0), axis=1, keepdims=True)

    first = column(table[0:1, :].astype(jnp.float32))
    second = column(table[1:2, :].astype(jnp.float32))
    square = (2 * channels, 2 * channels)
    diagonal = jnp.where(rows_of(square) == cols_of(square), angular[0], 0.0)
    mono = column(jnp.sum(diagonal, axis=0, keepdims=True))
    return 0.5 * first * (first + 1.0), 0.5 * second * (second + 1.0), mono


def kernel(
    n_rad, raw_hbm, tile_elems, widths_hbm, kin_hbm, rtwo_hbm, angular_hbm, table_hbm, out,
    raw, widths, kin_v, rtwo, angular, table, l_sem, full, next_in, below, spill, count, counts, kin, acc,
    c_send, c_recv, k_send, k_recv, e_send, e_recv,
):
    local_rows, channels, width_two = acc.shape[1:]
    lane_tiles = width_two // 128
    pitch = local_rows * lane_tiles * 2
    me_rad = lax.axis_index("rad")
    me_chan = lax.axis_index("chan")
    partner = 1 - me_chan
    rad_of = [lax.rem(me_rad + k, n_rad) for k in range(n_rad)]

    def place(x, row, tile):
        return pl.ds((row * lane_tiles + tile) * 2 + x, channels, stride=pitch)

    loads = []
    for source, target in (
        (raw_hbm.at[:, pl.ds(0, RAW_HEAD)], raw.at[:, pl.ds(0, RAW_HEAD)]),
        (raw_hbm.at[:, pl.ds(RAW_HEAD, pitch - RAW_HEAD)], raw.at[:, pl.ds(RAW_HEAD, pitch - RAW_HEAD)]),
        (kin_hbm, kin_v), (rtwo_hbm, rtwo), (angular_hbm, angular), (table_hbm, table), (widths_hbm, widths),
    ):
        load = pltpu.make_async_copy(source, target, l_sem.at[len(loads)])
        load.start()
        loads.append(load)
    barrier = pltpu.get_barrier_semaphore()
    pl.semaphore_signal(barrier, inc=1, device_id={"chan": partner}, device_id_type=MESH)
    for k in range(1, n_rad):
        pl.semaphore_signal(barrier, inc=1, device_id={"rad": rad_of[k]}, device_id_type=MESH)
    count[...] = jnp.full(count.shape, tile_elems[0], jnp.int32)

    def widen(begin, end):
        for c in range(channels):
            out[c * pitch + begin:c * pitch + end, :] = raw[c, begin:end, :].astype(jnp.float32)

    def unpack(g):
        for row in range(g * PTS, (g + 1) * PTS):
            for x in range(2):
                for tile in range(lane_tiles):
                    full[x, row, 0:channels, tile * 128:(tile + 1) * 128] = out[
                        place(x, row, tile), :].astype(jnp.bfloat16)

    loads[0].wait()
    widen(0, RAW_HEAD)
    unpack(0)
    pl.semaphore_wait(barrier, n_rad)
    count_copies = []
    for k in range(1, n_rad):
        copy = pltpu.make_async_remote_copy(
            src_ref=count, dst_ref=counts.at[k], send_sem=k_send.at[k], recv_sem=k_recv.at[k],
            device_id={"rad": rad_of[k]}, device_id_type=MESH)
        copy.start()
        count_copies.append(copy)
    edge_copies = []
    for x in range(2):
        copy = pltpu.make_async_remote_copy(
            src_ref=full.at[x, 0, pl.ds(0, channels)], dst_ref=next_in.at[x], send_sem=e_send.at[x],
            recv_sem=e_recv.at[x], device_id={"rad": rad_of[n_rad - 1]}, device_id_type=MESH)
        copy.start()
        edge_copies.append(copy)
    field_copies = {}
    for g in range(SLOTS):
        if g > 0:
            loads[1].wait()
            widen(RAW_HEAD, pitch)
            unpack(g)
        for x in range(2):
            copy = pltpu.make_async_remote_copy(
                src_ref=full.at[x, pl.ds(g * PTS, PTS), pl.ds(0, channels)],
                dst_ref=full.at[x, pl.ds(g * PTS, PTS), pl.ds(channels, channels)],
                send_sem=c_send.at[x, g], recv_sem=c_recv.at[x, g],
                device_id={"chan": partner}, device_id_type=MESH)
            copy.start()
            field_copies[x, g] = copy

    loads[2].wait()
    k_high, k_low = kinetic_parts(kin_v[...])
    k_high, k_low = k_high[:, :PTS * 16], k_low[:, :PTS * 16]
    for g in range(SLOTS):
        for x in range(2):
            for cb in range(channels // 16):
                block = full[x, g * PTS:(g + 1) * PTS, cb * 16:(cb + 1) * 16, :].reshape(PTS * 16, width_two)
                res = mm(k_high, block) + mm(k_low, block)
                kin[x, g, :, cb * 16:(cb + 1) * 16, :] = res.reshape(16, 16, width_two)

    own_count = count[0:1, 0:1]
    two_slots = own_count >= 2
    for x in range(2):
        spill[x] = jnp.where(two_slots, kin[x, 1, PTS], kin[x, 0, PTS]).astype(jnp.bfloat16)
        copy = pltpu.make_async_remote_copy(
            src_ref=spill.at[x], dst_ref=below.at[x], send_sem=e_send.at[2 + x], recv_sem=e_recv.at[2 + x],
            device_id={"rad": rad_of[1]}, device_id_type=MESH)
        copy.start()
        edge_copies.append(copy)

    loads[3].wait()
    r_high, r_low = two_parts(rtwo[...])
    for g in range(SLOTS):
        for x in range(2):
            for p0, size in ((0, 8), (8, 7)):
                rows = pl.ds(g * PTS + p0, size)
                block = full[x, rows, 0:channels, :].reshape(size * channels, width_two)
                acc[x, rows] = (mm(block, r_high) + mm(block, r_low)).reshape(size, channels, width_two)
    for load in loads[4:]:
        load.wait()
    m_high, m_low = channel_parts(table, angular, me_chan, channels, 4)
    first_l, second_l, mono = own_columns(table, angular, me_chan, channels)

    for copy in count_copies:
        copy.wait()
    offset = jnp.zeros((1, 1), jnp.int32)
    for k in range(1, n_rad):
        offset = offset + jnp.where(k <= me_rad, counts[k, 0:1, 0:1], 0)
    element = cols_of(widths.shape)
    all_widths = widths[...]

    def width_at(index):
        found = jnp.sum(jnp.where(element == index, all_widths, 0.0), axis=1, keepdims=True)
        return jnp.where(found > 0.0, found, 1.0)

    r_two = inner_radius + radial_step * cols_of((1, width_two)).astype(jnp.float32)
    inv_two = 1.0 / r_two
    base = second_l * (inv_two * inv_two) - charge * inv_two
    point = rows_of((16, 1))
    fractions = jnp.zeros((16, 1), jnp.float32)
    for p in range(1, 16):
        fractions = jnp.where(point == p, 0.5 * (1.0 - math.cos(math.pi * p / PTS)), fractions)

    for copy in edge_copies:
        copy.wait()
    inv_below = 1.0 / width_at(offset - 1)
    inv_below = jnp.where(me_rad > 0, inv_below * inv_below, 0.0)
    corner = kin_v[PTS:PTS + 1, PTS:PTS + 1]
    above = [jnp.where(me_rad < n_rad - 1, next_in[x].astype(jnp.float32), 0.0) for x in range(2)]
    inv_first = 1.0 / width_at(offset)
    inv_first = inv_first * inv_first
    for g in range(SLOTS):
        slot_width = width_at(offset + g)
        inv_w2 = 1.0 / slot_width
        inv_w2 = inv_w2 * inv_w2
        start = jnp.sum(jnp.where(element < offset + g, all_widths, 0.0), axis=1, keepdims=True)
        r_one = inner_radius + start + slot_width * fractions
        inv_one = 1.0 / r_one
        inv_far = 1.0 / jnp.maximum(r_one, r_two)
        weight = jnp.minimum(r_one, r_two) * inv_far * inv_far
        live = own_count > g
        after = []
        for x in range(2):
            field_copies[x, g].wait()
            if g == 0:
                row = jnp.where(two_slots, full[x, PTS, 0:channels, :].astype(jnp.float32), above[x])
            else:
                row = above[x]
            after.append(row * inv_w2)
        for p0, size in ((0, 4), (4, 4), (8, 4), (12, 3)):
            used = (slice(0, size * channels), slice(0, size * 2 * channels))
            for x in range(2):
                block = full[x, pl.ds(g * PTS + p0, size)].reshape(size * 2 * channels, width_two)
                mix = mm(m_high[used], block) + mm(m_low[used], block)
                for i in range(size):
                    q = p0 + i
                    row = g * PTS + q
                    mine_q = full[x, row, 0:channels, :].astype(jnp.float32)
                    potential = base + mono * inv_far[q:q + 1, :] + (
                        first_l * (inv_one[q:q + 1] * inv_one[q:q + 1]) - charge * inv_one[q:q + 1])
                    total = acc[x, row] + kin[x, g, q] * inv_w2 + kin_v[q:q + 1, PTS:PTS + 1] * after[x]
                    total = total + potential * mine_q
                    total = total + weight[q:q + 1, :] * mix[i * channels:(i + 1) * channels]
                    if q == 0:
                        if g == 0:
                            total = total + (below[x].astype(jnp.float32) + corner * mine_q) * inv_below
                        else:
                            total = total + (kin[x, 0, PTS] + corner * mine_q) * inv_first
                    step = time_step if x == 1 else -time_step
                    result = full[1 - x, row, 0:channels, :].astype(jnp.float32) + step * total
                    result = jnp.where(live, result, 0.0)
                    for tile in range(lane_tiles):
                        out[place(1 - x, row, tile), :] = result[:, tile * 128:(tile + 1) * 128]


def per_device(n_rad, wave, tile_elems, element_width, element_kinetic, radial_two, angular, channel_table):
    channels, _, rows, width_two = wave.shape
    tiles = width_two // 128
    raw = wave.reshape(channels, 2, rows, tiles, 128).transpose(0, 2, 3, 1, 4)
    raw = raw.reshape(channels, -1, 128)
    hbm = pl.BlockSpec(memory_space=pltpu.HBM)
    smem = pl.BlockSpec(memory_space=pltpu.SMEM)
    edge = pltpu.VMEM((2, channels, width_two), jnp.bfloat16)
    evolved = pl.pallas_call(
        functools.partial(kernel, n_rad),
        out_shape=pltpu.VMEM((raw.shape[0] * raw.shape[1], 128), jnp.float32),
        in_specs=[hbm, smem, hbm, hbm, hbm, hbm, hbm],
        out_specs=pl.BlockSpec(memory_space=pltpu.VMEM),
        scratch_shapes=[
            pltpu.VMEM(raw.shape, jnp.bfloat16),
            pltpu.VMEM((1, element_width.shape[0]), jnp.float32),
            pltpu.VMEM(element_kinetic.shape, jnp.float32),
            pltpu.VMEM(radial_two.shape, jnp.float32),
            pltpu.VMEM(angular.shape, jnp.float32),
            pltpu.VMEM(channel_table.shape[::-1], jnp.int32),
            pltpu.SemaphoreType.DMA((7,)),
            pltpu.VMEM((2, rows, 2 * channels, width_two), jnp.bfloat16),
            edge, edge, edge,
            pltpu.VMEM((8, 128), jnp.int32),
            pltpu.VMEM((n_rad, 8, 128), jnp.int32),
            pltpu.VMEM((2, SLOTS, 16, channels, width_two), jnp.float32),
            pltpu.VMEM((2, rows, channels, width_two), jnp.float32),
            pltpu.SemaphoreType.DMA((2, SLOTS)),
            pltpu.SemaphoreType.DMA((2, SLOTS)),
            pltpu.SemaphoreType.DMA((n_rad,)),
            pltpu.SemaphoreType.DMA((n_rad,)),
            pltpu.SemaphoreType.DMA((4,)),
            pltpu.SemaphoreType.DMA((4,)),
        ],
        compiler_params=pltpu.CompilerParams(
            collective_id=0, has_side_effects=True, vmem_limit_bytes=58 * 1024 * 1024),
        cost_estimate=pl.CostEstimate(flops=6_000_000_000, bytes_accessed=10_000_000, transcendentals=0),
    )(raw, tile_elems, element_width[None, :], element_kinetic, radial_two, angular,
      channel_table.T)
    evolved = evolved.reshape(channels, rows, tiles, 2, 128).transpose(0, 3, 1, 2, 4)
    return evolved.reshape(wave.shape)


def solution(mesh):
    in_specs = (P("chan", None, "rad", "grp"), P(("grp", "rad")), P("grp"), P(), P(), P(), P())
    out_specs = P("chan", None, "rad", "grp")
    return jax.shard_map(
        functools.partial(per_device, mesh.shape["rad"]), mesh=mesh, in_specs=in_specs,
        out_specs=out_specs, check_vma=False)
```

```python
import functools
import math

import jax
import jax.numpy as jnp
from jax import lax
from jax.experimental import pallas as pl
from jax.experimental.pallas import tpu as pltpu
from jax.sharding import PartitionSpec as P

PTS = 15
SLOTS = 2
RAW_HEAD = 128
MESH = pl.DeviceIdType.MESH
highest = lax.Precision.HIGHEST
charge = 2.0
inner_radius = 4.0
radial_step = 0.1
time_step = 0.1


def mm(a, b):
    return jnp.dot(a, b, preferred_element_type=jnp.float32)


def two_parts(a):
    high = a.astype(jnp.bfloat16)
    return high, (a - high.astype(jnp.float32)).astype(jnp.bfloat16)


def one_hot(shape, index):
    return (index == lax.broadcasted_iota(jnp.int32, shape, 1)).astype(jnp.float32)


def rows_of(shape):
    return lax.broadcasted_iota(jnp.int32, shape, 0)


def cols_of(shape):
    return lax.broadcasted_iota(jnp.int32, shape, 1)


def spread(pick_rows, matrix, pick_cols):
    first = jnp.dot(pick_rows, matrix, precision=highest, preferred_element_type=jnp.float32)
    return lax.dot_general(
        first, pick_cols, (((1,), (1,)), ((), ())), precision=highest, preferred_element_type=jnp.float32)


def kinetic_parts(kinetic):
    pick = one_hot((256, 16), rows_of((256, 16)) // 16)
    keep = rows_of((256, 256)) % 16 == cols_of((256, 256)) % 16
    return two_parts(jnp.where(keep, spread(pick, kinetic, pick), 0.0))


def channel_parts(table, angular, me, channels, points):
    every = 2 * channels
    square = (every, every)
    eye = rows_of(square) == cols_of(square)
    keep = None
    for electron in range(2):
        row = table[electron:electron + 1, :].astype(jnp.float32)
        column = jnp.sum(jnp.where(eye, row, 0.0), axis=1, keepdims=True)
        apart = jnp.abs(column - row) == 1.0
        keep = apart if keep is None else keep & apart
    turned = lax.dot_general(
        eye.astype(jnp.float32), angular[1], (((1,), (1,)), ((), ())), precision=highest,
        preferred_element_type=jnp.float32)
    matrix = jnp.where(keep, 0.5 * (angular[1] + turned), 0.0)
    out_rows, in_rows = points * channels, points * every
    pick_r = one_hot((out_rows, every), me * channels + rows_of((out_rows, every)) % channels)
    pick_c = one_hot((in_rows, every), (rows_of((in_rows, every)) + me * channels) % every)
    same = rows_of((out_rows, in_rows)) // channels == cols_of((out_rows, in_rows)) // every
    return two_parts(jnp.where(same, spread(pick_r, matrix, pick_c), 0.0))


def own_columns(table, angular, me, channels):
    shape = (channels, 2 * channels)
    mine = rows_of(shape) + me * channels == cols_of(shape)

    def column(row):
        return jnp.sum(jnp.where(mine, row, 0.0), axis=1, keepdims=True)

    first = column(table[0:1, :].astype(jnp.float32))
    second = column(table[1:2, :].astype(jnp.float32))
    square = (2 * channels, 2 * channels)
    diagonal = jnp.where(rows_of(square) == cols_of(square), angular[0], 0.0)
    mono = column(jnp.sum(diagonal, axis=0, keepdims=True))
    return 0.5 * first * (first + 1.0), 0.5 * second * (second + 1.0), mono


def kernel(
    n_rad, raw_hbm, tile_elems, widths_hbm, kin_hbm, rtwo_hbm, angular_hbm, table_hbm, out,
    raw, widths, kin_v, rtwo, angular, table, l_sem, full, next_in, below, spill, count, counts, kin, acc,
    c_send, c_recv, k_send, k_recv, e_send, e_recv,
):
    local_rows, channels, width_two = acc.shape[1:]
    lane_tiles = width_two // 128
    pitch = local_rows * lane_tiles * 2
    me_rad = lax.axis_index("rad")
    me_chan = lax.axis_index("chan")
    partner = 1 - me_chan
    rad_of = [lax.rem(me_rad + k, n_rad) for k in range(n_rad)]

    def place(x, row, tile):
        return pl.ds((row * lane_tiles + tile) * 2 + x, channels, stride=pitch)

    tail = pitch - RAW_HEAD
    loads = [pltpu.make_async_copy(source, target, l_sem.at[i]) for i, (source, target) in enumerate((
        (raw_hbm.at[:, pl.ds(0, RAW_HEAD)], raw.at[:, pl.ds(0, RAW_HEAD)]),
        (raw_hbm.at[:, pl.ds(RAW_HEAD, tail)], raw.at[:, pl.ds(RAW_HEAD, tail)]),
        (kin_hbm, kin_v), (rtwo_hbm, rtwo), (angular_hbm, angular), (table_hbm, table), (widths_hbm, widths)))]
    for i in (2, 4, 5, 6, 0, 1, 3):
        loads[i].start()
    barrier = pltpu.get_barrier_semaphore()
    pl.semaphore_signal(barrier, inc=1, device_id={"chan": partner}, device_id_type=MESH)
    for k in range(1, n_rad):
        pl.semaphore_signal(barrier, inc=1, device_id={"rad": rad_of[k]}, device_id_type=MESH)
    count[...] = jnp.full(count.shape, tile_elems[0], jnp.int32)

    def widen(begin, end):
        for c in range(channels):
            out[c * pitch + begin:c * pitch + end, :] = raw[c, begin:end, :].astype(jnp.float32)

    def unpack(g):
        for row in range(g * PTS, (g + 1) * PTS):
            for x in range(2):
                for tile in range(lane_tiles):
                    full[x, row, 0:channels, tile * 128:(tile + 1) * 128] = out[
                        place(x, row, tile), :].astype(jnp.bfloat16)

    loads[2].wait()
    k_high, k_low = kinetic_parts(kin_v[...])
    k_high, k_low = k_high[:, :PTS * 16], k_low[:, :PTS * 16]
    for load in loads[4:]:
        load.wait()
    m_high, m_low = channel_parts(table, angular, me_chan, channels, 4)
    first_l, second_l, mono = own_columns(table, angular, me_chan, channels)
    loads[0].wait()
    widen(0, RAW_HEAD)
    unpack(0)
    pl.semaphore_wait(barrier, n_rad)
    count_copies = []
    for k in range(1, n_rad):
        copy = pltpu.make_async_remote_copy(
            src_ref=count, dst_ref=counts.at[k], send_sem=k_send.at[k], recv_sem=k_recv.at[k],
            device_id={"rad": rad_of[k]}, device_id_type=MESH)
        copy.start()
        count_copies.append(copy)
    edge_copies = []
    for x in range(2):
        copy = pltpu.make_async_remote_copy(
            src_ref=full.at[x, 0, pl.ds(0, channels)], dst_ref=next_in.at[x], send_sem=e_send.at[x],
            recv_sem=e_recv.at[x], device_id={"rad": rad_of[n_rad - 1]}, device_id_type=MESH)
        copy.start()
        edge_copies.append(copy)
    field_copies = {}
    for g in range(SLOTS):
        if g > 0:
            loads[1].wait()
            widen(RAW_HEAD, pitch)
            unpack(g)
        for x in range(2):
            copy = pltpu.make_async_remote_copy(
                src_ref=full.at[x, pl.ds(g * PTS, PTS), pl.ds(0, channels)],
                dst_ref=full.at[x, pl.ds(g * PTS, PTS), pl.ds(channels, channels)],
                send_sem=c_send.at[x, g], recv_sem=c_recv.at[x, g],
                device_id={"chan": partner}, device_id_type=MESH)
            copy.start()
            field_copies[x, g] = copy

    for g in range(SLOTS):
        for x in range(2):
            for cb in range(channels // 16):
                block = full[x, g * PTS:(g + 1) * PTS, cb * 16:(cb + 1) * 16, :].reshape(PTS * 16, width_two)
                res = mm(k_high, block) + mm(k_low, block)
                kin[x, g, :, cb * 16:(cb + 1) * 16, :] = res.reshape(16, 16, width_two)

    own_count = count[0:1, 0:1]
    two_slots = own_count >= 2
    for x in range(2):
        spill[x] = jnp.where(two_slots, kin[x, 1, PTS], kin[x, 0, PTS]).astype(jnp.bfloat16)
        copy = pltpu.make_async_remote_copy(
            src_ref=spill.at[x], dst_ref=below.at[x], send_sem=e_send.at[2 + x], recv_sem=e_recv.at[2 + x],
            device_id={"rad": rad_of[1]}, device_id_type=MESH)
        copy.start()
        edge_copies.append(copy)

    loads[3].wait()
    r_high, r_low = two_parts(rtwo[...])
    for g in range(SLOTS):
        for x in range(2):
            for p0, size in ((0, 8), (8, 7)):
                rows = pl.ds(g * PTS + p0, size)
                block = full[x, rows, 0:channels, :].reshape(size * channels, width_two)
                acc[x, rows] = (mm(block, r_high) + mm(block, r_low)).reshape(size, channels, width_two)

    for copy in count_copies:
        copy.wait()
    offset = jnp.zeros((1, 1), jnp.int32)
    for k in range(1, n_rad):
        offset = offset + jnp.where(k <= me_rad, counts[k, 0:1, 0:1], 0)
    element = cols_of(widths.shape)
    all_widths = widths[...]

    def width_at(index):
        found = jnp.sum(jnp.where(element == index, all_widths, 0.0), axis=1, keepdims=True)
        return jnp.where(found > 0.0, found, 1.0)

    r_two = inner_radius + radial_step * cols_of((1, width_two)).astype(jnp.float32)
    inv_two = 1.0 / r_two
    base = second_l * (inv_two * inv_two) - charge * inv_two
    point = rows_of((16, 1))
    fractions = jnp.zeros((16, 1), jnp.float32)
    for p in range(1, 16):
        fractions = jnp.where(point == p, 0.5 * (1.0 - math.cos(math.pi * p / PTS)), fractions)

    for copy in edge_copies:
        copy.wait()
    inv_below = 1.0 / width_at(offset - 1)
    inv_below = jnp.where(me_rad > 0, inv_below * inv_below, 0.0)
    corner = kin_v[PTS:PTS + 1, PTS:PTS + 1]
    above = [jnp.where(me_rad < n_rad - 1, next_in[x].astype(jnp.float32), 0.0) for x in range(2)]
    inv_first = 1.0 / width_at(offset)
    inv_first = inv_first * inv_first
    for g in range(SLOTS):
        slot_width = width_at(offset + g)
        inv_w2 = 1.0 / slot_width
        inv_w2 = inv_w2 * inv_w2
        start = jnp.sum(jnp.where(element < offset + g, all_widths, 0.0), axis=1, keepdims=True)
        r_one = inner_radius + start + slot_width * fractions
        inv_one = 1.0 / r_one
        inv_far = 1.0 / jnp.maximum(r_one, r_two)
        weight = jnp.minimum(r_one, r_two) * inv_far * inv_far
        live = own_count > g
        after = []
        for x in range(2):
            field_copies[x, g].wait()
            if g == 0:
                row = jnp.where(two_slots, full[x, PTS, 0:channels, :].astype(jnp.float32), above[x])
            else:
                row = above[x]
            after.append(row * inv_w2)
        for p0, size in ((0, 4), (4, 4), (8, 4), (12, 3)):
            used = (slice(0, size * channels), slice(0, size * 2 * channels))
            for x in range(2):
                block = full[x, pl.ds(g * PTS + p0, size)].reshape(size * 2 * channels, width_two)
                mix = mm(m_high[used], block) + mm(m_low[used], block)
                for i in range(size):
                    q = p0 + i
                    row = g * PTS + q
                    mine_q = full[x, row, 0:channels, :].astype(jnp.float32)
                    potential = base + mono * inv_far[q:q + 1, :] + (
                        first_l * (inv_one[q:q + 1] * inv_one[q:q + 1]) - charge * inv_one[q:q + 1])
                    total = acc[x, row] + kin[x, g, q] * inv_w2 + kin_v[q:q + 1, PTS:PTS + 1] * after[x]
                    total = total + potential * mine_q
                    total = total + weight[q:q + 1, :] * mix[i * channels:(i + 1) * channels]
                    if q == 0:
                        if g == 0:
                            total = total + (below[x].astype(jnp.float32) + corner * mine_q) * inv_below
                        else:
                            total = total + (kin[x, 0, PTS] + corner * mine_q) * inv_first
                    step = time_step if x == 1 else -time_step
                    result = full[1 - x, row, 0:channels, :].astype(jnp.float32) + step * total
                    result = jnp.where(live, result, 0.0)
                    for tile in range(lane_tiles):
                        out[place(1 - x, row, tile), :] = result[:, tile * 128:(tile + 1) * 128]


def per_device(n_rad, wave, tile_elems, element_width, element_kinetic, radial_two, angular, channel_table):
    channels, _, rows, width_two = wave.shape
    tiles = width_two // 128
    raw = wave.reshape(channels, 2, rows, tiles, 128).transpose(0, 2, 3, 1, 4)
    raw = raw.reshape(channels, -1, 128)
    hbm = pl.BlockSpec(memory_space=pltpu.HBM)
    smem = pl.BlockSpec(memory_space=pltpu.SMEM)
    edge = pltpu.VMEM((2, channels, width_two), jnp.bfloat16)
    evolved = pl.pallas_call(
        functools.partial(kernel, n_rad),
        out_shape=pltpu.VMEM((raw.shape[0] * raw.shape[1], 128), jnp.float32),
        in_specs=[hbm, smem, hbm, hbm, hbm, hbm, hbm],
        out_specs=pl.BlockSpec(memory_space=pltpu.VMEM),
        scratch_shapes=[
            pltpu.VMEM(raw.shape, jnp.bfloat16),
            pltpu.VMEM((1, element_width.shape[0]), jnp.float32),
            pltpu.VMEM(element_kinetic.shape, jnp.float32),
            pltpu.VMEM(radial_two.shape, jnp.float32),
            pltpu.VMEM(angular.shape, jnp.float32),
            pltpu.VMEM(channel_table.shape[::-1], jnp.int32),
            pltpu.SemaphoreType.DMA((7,)),
            pltpu.VMEM((2, rows, 2 * channels, width_two), jnp.bfloat16),
            edge, edge, edge,
            pltpu.VMEM((8, 128), jnp.int32),
            pltpu.VMEM((n_rad, 8, 128), jnp.int32),
            pltpu.VMEM((2, SLOTS, 16, channels, width_two), jnp.float32),
            pltpu.VMEM((2, rows, channels, width_two), jnp.float32),
            pltpu.SemaphoreType.DMA((2, SLOTS)),
            pltpu.SemaphoreType.DMA((2, SLOTS)),
            pltpu.SemaphoreType.DMA((n_rad,)),
            pltpu.SemaphoreType.DMA((n_rad,)),
            pltpu.SemaphoreType.DMA((4,)),
            pltpu.SemaphoreType.DMA((4,)),
        ],
        compiler_params=pltpu.CompilerParams(
            collective_id=0, has_side_effects=True, vmem_limit_bytes=58 * 1024 * 1024),
        cost_estimate=pl.CostEstimate(flops=6_000_000_000, bytes_accessed=10_000_000, transcendentals=0),
    )(raw, tile_elems, element_width[None, :], element_kinetic, radial_two, angular,
      channel_table.T)
    evolved = evolved.reshape(channels, rows, tiles, 2, 128).transpose(0, 3, 1, 2, 4)
    return evolved.reshape(wave.shape)


def solution(mesh):
    in_specs = (P("chan", None, "rad", "grp"), P(("grp", "rad")), P("grp"), P(), P(), P(), P())
    out_specs = P("chan", None, "rad", "grp")
    return jax.shard_map(
        functools.partial(per_device, mesh.shape["rad"]), mesh=mesh, in_specs=in_specs,
        out_specs=out_specs, check_vma=False)
```
